768 devices in a mesh: row: 8 (over z_hi, core), col: 96 (over x, y, z_lo).
Axes of the slice: x: 4, y: 8, z: 12 (z_hi: 4, z_lo: 3; z = z_hi * 3 + z_lo), core: 2. Of those that a mesh axis runs over, the one named last changes fastest.
Arguments:
- features: bfloat16 [24576, 256], P(('row', 'col')), may hold values from -6 to 6
- weight: bfloat16 [256, 256], replicated, may hold values from -0.375 to 0.375
- out_counts: int32 [24576], P(('row', 'col')), may hold values from 32 to 256
- in_counts: int32 [24576], P(('col', 'row')), may hold values from 32 to 256
- tile_mask: int32 [96, 8, 36, 128, 128], P('col', 'row'), may hold values 0 or 1
- tile_pos: int32 [96, 8, 36], P('col', 'row'), may hold values from 0 to 47, as said below
- tile_count: int32 [96, 8], P('col', 'row'), may hold values from 1 to 36, as said below
- cotangent: bfloat16 [24576, 256], P(('col', 'row')), may hold values from -6 to 6
Outputs:
- output: bfloat16 [24576, 256], P(('col', 'row'))
- grad_features: bfloat16 [24576, 256], P(('row', 'col'))
- grad_weight: float32 [256, 256], replicated
The draws below stay inside these ranges and needn't reach their ends.
Inputs may be any that keep to these rules, and one draw needn't show every extreme that they name: `tile_pos`: slots of one device name distinct positions. `tile_count`: some device has all 36 slots live.
All inputs are finite; a program needn't handle non-finite values. No bound on the sum of `tile_mask` on one device may be relied on, other than what follows from the above.
Results may differ from the reference program's by a relative error of at most 0.015.
Values may be sent and summed in bfloat16 or wider, within the bound.
No kernel may reach another device: no remote copies, remote signals or barrier semaphores. Data moves between devices by JAX's collectives and lax.ppermute only.
A program may use at most 32 MiB of HBM per device.

```python
import jax
import jax.numpy as jnp
from jax import lax

F = 256
TILE = 128
DEG_MAX = 256
NODES = 24576
RB = 256
CB = 3072
POS = 48
TILES_DEV = 36
N_ROW = 8
N_COL = 96


def draw_tile_pos(key, part):
    key = jax.random.fold_in(key, 11)
    keys = jax.random.split(key, N_COL * N_ROW)
    places = jax.vmap(lambda single: jax.random.permutation(single, POS)[:TILES_DEV])(keys)
    return places.reshape(N_COL, N_ROW, TILES_DEV).astype(jnp.int32)


def draw_tile_count(key, part):
    key = jax.random.fold_in(key, 23)
    first, second, third = jax.random.split(key, 3)
    left = jax.random.randint(first, (N_COL * N_ROW,), 0, TILES_DEV + 1)
    right = jax.random.randint(second, (N_COL * N_ROW,), 0, TILES_DEV + 1)
    counts = 1 + left * right // (TILES_DEV + 1)
    fullest = jax.random.randint(third, (), 0, N_COL * N_ROW)
    counts = counts.at[fullest].set(TILES_DEV)
    return counts.reshape(N_COL, N_ROW).astype(jnp.int32)


def with_ends(result, own_key, least, largest):
    spot = [jax.random.randint(jax.random.fold_in(own_key, axis), (), 0, length) for axis, length in enumerate(result.shape)]
    main_axis = result.shape.index(max(result.shape))
    beside = spot[:main_axis] + [(spot[main_axis] + 1) % result.shape[main_axis]] + spot[main_axis + 1:]
    return result.at[tuple(spot)].set(least).at[tuple(beside)].set(largest)


def steps_of(key, extent, shards, smallest, largest):
    loudness = 1.0
    for dim, parts in shards:
        heights = jax.random.uniform(jax.random.fold_in(jax.random.fold_in(key, 6), dim), (parts,), jnp.float32, smallest / len(shards), largest / len(shards))
        loudness = loudness * jnp.repeat(jnp.exp(heights), extent[dim] // parts).reshape((-1,) + (1,) * (len(extent) - 1 - dim))
    return loudness


def gaussian(own_key, extent, deviation, reach, shards=(), kind=jnp.bfloat16):
    level = steps_of(own_key, extent, shards, -0.22, 0.18) if shards else 1.0
    values = jax.random.normal(own_key, extent, jnp.float32) * deviation * level
    return jnp.minimum(jnp.maximum(values, -reach), reach).astype(kind)


def setup_inputs(seed: int = 0) -> dict:
    arg_keys = jax.random.split(jax.random.key(seed), 9)
    features = gaussian(arg_keys[0], (NODES, F), 1.0, 6.0, ((0, 768),))
    weight = gaussian(arg_keys[1], (F, F), F ** -0.5, 0.375)
    out_counts = with_ends(jax.random.randint(arg_keys[2], (NODES,), TILE // 4, DEG_MAX + 1), jax.random.fold_in(arg_keys[2], 1), TILE // 4, DEG_MAX).astype(jnp.int32)
    in_counts = with_ends(jax.random.randint(arg_keys[3], (NODES,), TILE // 4, DEG_MAX + 1), jax.random.fold_in(arg_keys[3], 1), TILE // 4, DEG_MAX).astype(jnp.int32)
    tile_mask = with_ends((jax.random.randint(arg_keys[4], (N_COL, N_ROW, TILES_DEV, TILE, TILE), 0, 8) < 1).astype(jnp.int32), jax.random.fold_in(arg_keys[4], 1), 0, 1)
    tile_pos = draw_tile_pos(jax.random.fold_in(arg_keys[8], 71), 0)
    tile_count = draw_tile_count(jax.random.fold_in(arg_keys[8], 71), 0)
    cotangent = gaussian(arg_keys[7], (NODES, F), 1.0, 6.0, ((0, 768),))
    return dict(features=features, weight=weight, out_counts=out_counts, in_counts=in_counts, tile_mask=tile_mask, tile_pos=tile_pos, tile_count=tile_count, cotangent=cotangent)


def reference(features, weight, out_counts, in_counts, tile_mask, tile_pos, tile_count, cotangent):
    tile_cols = CB // TILE
    tile_rows = RB // TILE
    out_scale = lax.rsqrt(out_counts.astype(jnp.float32))
    in_scale = lax.rsqrt(in_counts.astype(jnp.float32))
    source = (jnp.dot(features, weight, preferred_element_type=jnp.float32) * out_scale[:, None]).astype(jnp.bfloat16)
    scaled = (cotangent.astype(jnp.float32) * in_scale[:, None]).astype(jnp.bfloat16)
    source_tiles = source.reshape(NODES // TILE, TILE, F)
    scaled_tiles = scaled.reshape(NODES // TILE, TILE, F)
    masks = tile_mask.reshape(N_COL * N_ROW, TILES_DEV, TILE, TILE)
    places = tile_pos.reshape(N_COL * N_ROW, TILES_DEV)
    counts = tile_count.reshape(N_COL * N_ROW)
    devices = jnp.arange(N_COL * N_ROW, dtype=jnp.int32)
    slots = jnp.arange(TILES_DEV, dtype=jnp.int32)

    def advance(carry, items):
        forward, backward = carry
        piece, place, number, device = items
        col_index = device // N_ROW
        row_index = device % N_ROW
        active = slots < number
        blocks = jnp.where(active[:, None, None], piece, 0).astype(jnp.float32)
        global_rows = (col_index * tile_rows + place // tile_cols).astype(jnp.int32)
        global_cols = (row_index * tile_cols + place % tile_cols).astype(jnp.int32)
        forward = forward.at[global_rows].add(jnp.einsum('tij,tjf->tif', blocks, source_tiles[global_cols].astype(jnp.float32)))
        backward = backward.at[global_cols].add(jnp.einsum('tij,tif->tjf', blocks, scaled_tiles[global_rows].astype(jnp.float32)))
        return ((forward, backward), None)
    empty = jnp.zeros((NODES // TILE, TILE, F), jnp.float32)
    (forward, backward), _ = lax.scan(advance, (empty, empty), (masks, places, counts, devices))
    output = (forward.reshape(NODES, F) * in_scale[:, None]).astype(jnp.bfloat16)
    back_agg = (backward.reshape(NODES, F) * out_scale[:, None]).astype(jnp.bfloat16)
    grad_features = jnp.dot(back_agg, weight.T, preferred_element_type=jnp.float32).astype(jnp.bfloat16)
    grad_weight = jnp.dot(features.T, back_agg, preferred_element_type=jnp.float32)
    return (output, grad_features, grad_weight)
```

```python
import jax
import jax.numpy as jnp
from jax import lax
from jax.experimental import pallas as pl
from jax.experimental.pallas import tpu as pltpu
from jax.sharding import Mesh, PartitionSpec as P

TILE = 128
STEP = 6
ROW = ("zh", "core")
COL = ("x", "y", "zl")
SIZES = {"zh": 4, "core": 2, "x": 4, "y": 8, "zl": 3}


def place_tiles(count_ref, place_ref, mask_ref, dense_ref):
    step = pl.program_id(0)
    tile_cols = dense_ref.shape[1] // TILE

    @pl.when(step == 0)
    def _():
        dense_ref[...] = jnp.zeros_like(dense_ref)

    for inner in range(STEP):
        slot = step * STEP + inner

        @pl.when(slot < count_ref[0])
        def _():
            place = place_ref[slot]
            row = pl.multiple_of(place // tile_cols * TILE, TILE)
            col = pl.multiple_of(place % tile_cols * TILE, TILE)
            block = mask_ref[inner].astype(jnp.float32).astype(jnp.bfloat16)
            dense_ref[pl.ds(row, TILE), pl.ds(col, TILE)] = block


def dense_block(masks, places, count, rows, cols):
    slots = masks.shape[0]
    return pl.pallas_call(
        place_tiles,
        out_shape=jax.ShapeDtypeStruct((rows, cols), jnp.bfloat16),
        grid_spec=pltpu.PrefetchScalarGridSpec(
            num_scalar_prefetch=2,
            grid=(slots // STEP,),
            in_specs=[pl.BlockSpec((STEP, TILE, TILE), lambda i, n, p: (i, 0, 0))],
            out_specs=pl.BlockSpec((rows, cols), lambda i, n, p: (0, 0)),
        ),
        compiler_params=pltpu.CompilerParams(vmem_limit_bytes=16 * 1024 * 1024),
        cost_estimate=pl.CostEstimate(
            flops=slots * TILE * TILE,
            bytes_accessed=slots * TILE * TILE * 4 + rows * cols * 2,
            transcendentals=0,
        ),
        name="place_tiles",
    )(count, places, masks)


def size_of(axes):
    size = 1
    for axis in axes:
        size *= SIZES[axis]
    return size


def spread(piece, axes):
    count = size_of(axes)
    return lax.all_to_all(jnp.broadcast_to(piece[None], (count, *piece.shape)), axes, 0, 0)


def swap(pieces, axes):
    return lax.all_to_all(pieces, axes, 0, 0)


def total(pieces):
    return jnp.sum(pieces.astype(jnp.float32), axis=0)


def shifted(piece, axis, step):
    size = SIZES[axis]
    return lax.ppermute(piece, axis, [(i, (i + step) % size) for i in range(size)])


def gather_by_shifts(piece, axis, dim):
    size, me = SIZES[axis], lax.axis_index(axis)
    shape = piece.shape[:dim] + (size,) + piece.shape[dim:]
    whole = jnp.zeros(shape, piece.dtype)
    for step in range(size):
        block = piece if step == 0 else shifted(piece, axis, step)
        whole = lax.dynamic_update_index_in_dim(whole, block, (me + size - step) % size, dim)
    return whole


def block_of(pieces, axis, step, dim):
    place = (lax.axis_index(axis) + step) % SIZES[axis]
    return lax.dynamic_index_in_dim(pieces, place, dim, keepdims=False)


def scatter_by_shifts(pieces, axis):
    whole = block_of(pieces, axis, 0, 0).astype(jnp.float32)
    for step in range(1, SIZES[axis]):
        block = shifted(block_of(pieces, axis, step, 0), axis, step)
        whole = whole + block.astype(jnp.float32)
    return whole.astype(pieces.dtype)


def beside(pieces, block):
    return jnp.concatenate(
        [pieces, jnp.broadcast_to(block[None], (pieces.shape[0], *block.shape))], axis=1
    )


def local(features, weight, out_counts, in_counts, tile_mask, tile_pos, tile_count, cotangent):
    bf16, f32 = jnp.bfloat16, jnp.float32
    mine, width = features.shape
    rows = mine * size_of(ROW)
    cols = mine * size_of(COL)
    out_scale = lax.rsqrt(out_counts.astype(f32))[:, None]
    in_scale = lax.rsqrt(in_counts.astype(f32))[:, None]
    scaled_features = (features.astype(f32) * out_scale).astype(bf16)
    scaled = (cotangent.astype(f32) * in_scale).astype(bf16)

    near = spread(scaled_features, ("y", "zl")).reshape(-1, width)
    across = gather_by_shifts(scaled, "zh", 0)
    near, across = lax.optimization_barrier((near, across))
    targets = gather_by_shifts(across, "core", 1).reshape(rows, width)
    dense = dense_block(tile_mask[0, 0], tile_pos[0, 0], tile_count[0], rows, cols)
    sources = spread(near, ("x",)).reshape(cols, width)

    backward = lax.dot_general(
        dense, targets, (((0,), (0,)), ((), ())), preferred_element_type=f32
    ).astype(bf16)
    thirds = backward.reshape(-1, SIZES["zl"], mine, width)
    kept, second, third = (block_of(thirds, "zl", step, 1) for step in range(3))

    forward = jnp.dot(dense, sources, preferred_element_type=f32).astype(bf16)
    outer = lax.dot_general(
        forward, targets, (((0,), (0,)), ((), ())), preferred_element_type=f32
    ).astype(bf16)
    outer = total(swap(outer.reshape(SIZES["y"], -1, width), ("y",))).astype(bf16)
    outer, second = lax.optimization_barrier((outer, shifted(second, "zl", 1)))
    outer = total(spread(outer, ("x", "zl"))).astype(bf16)
    outer, third = lax.optimization_barrier((outer, shifted(third, "zl", 2)))
    part = (kept.astype(f32) + second.astype(f32) + third.astype(f32)).astype(bf16)
    part = scatter_by_shifts(part.reshape(SIZES["x"], -1, mine, width), "x")
    both = total(swap(beside(forward.reshape(-1, mine, width), outer), ROW))
    forward_mine, outer = both[:mine], both[mine:].astype(bf16)
    output = (
        jnp.dot(forward_mine.astype(bf16), weight, preferred_element_type=f32) * in_scale
    ).astype(bf16)

    last = swap(beside(part, outer), ("y",))
    grad_weight = last[:, mine:].reshape(width, width).astype(f32)
    back_agg = (total(last[:, :mine]) * out_scale).astype(bf16)
    grad_features = lax.dot_general(
        back_agg, weight, (((1,), (1,)), ((), ())), preferred_element_type=f32
    ).astype(bf16)
    return (output, grad_features, grad_weight)


def solution(mesh):
    fine = Mesh(mesh.devices.reshape(tuple(SIZES.values())), tuple(SIZES))
    by_row, by_col = ROW + COL, COL + ROW
    placed = (
        P(by_row, None),
        P(),
        P(by_row),
        P(by_col),
        P(COL, ROW, None, None, None),
        P(COL, ROW, None),
        P(COL, ROW),
        P(by_col, None),
    )
    return jax.shard_map(
        local,
        mesh=fine,
        in_specs=placed,
        out_specs=(P(by_col, None), P(by_row, None), P()),
        check_vma=False,
    )
```

```python
import jax
import jax.numpy as jnp
from jax import lax
from jax.experimental import pallas as pl
from jax.experimental.pallas import tpu as pltpu
from jax.sharding import Mesh, PartitionSpec as P

TILE = 128
STEP = 6
ROW = ("zh", "core")
COL = ("x", "y", "zl")
SIZES = {"zh": 4, "core": 2, "x": 4, "y": 8, "zl": 3}


def place_tiles(count_ref, place_ref, mask_ref, dense_ref):
    step = pl.program_id(0)
    tile_cols = dense_ref.shape[1] // TILE

    @pl.when(step == 0)
    def _():
        dense_ref[...] = jnp.zeros_like(dense_ref)

    for inner in range(STEP):
        slot = step * STEP + inner

        @pl.when(slot < count_ref[0])
        def _():
            place = place_ref[slot]
            row = pl.multiple_of(place // tile_cols * TILE, TILE)
            col = pl.multiple_of(place % tile_cols * TILE, TILE)
            block = mask_ref[inner].astype(jnp.float32).astype(jnp.bfloat16)
            dense_ref[pl.ds(row, TILE), pl.ds(col, TILE)] = block


def scale_copies(count_ref, value_ref, copies_ref):
    nodes = value_ref.shape[0]
    scale = lax.rsqrt(count_ref[...].astype(jnp.float32))
    here = lax.broadcasted_iota(jnp.int32, (nodes, nodes), 0)
    there = lax.broadcasted_iota(jnp.int32, (nodes, nodes), 1)
    scale = jnp.broadcast_to(scale, (nodes, nodes))
    scale = jnp.sum(jnp.where(here == there, scale, 0.0), axis=1, keepdims=True)
    scaled = (value_ref[...].astype(jnp.float32) * scale).astype(copies_ref.dtype)
    for copy in range(copies_ref.shape[0]):
        copies_ref[copy] = scaled


def scaled_copies(values, counts, axes):
    return pl.pallas_call(
        scale_copies,
        out_shape=jax.ShapeDtypeStruct((size_of(axes), *values.shape), values.dtype),
        in_specs=[pl.BlockSpec(memory_space=pltpu.VMEM)] * 2,
        out_specs=pl.BlockSpec(memory_space=pltpu.VMEM),
        name="scale_copies",
    )(counts.reshape(1, -1), values)


def apply_dense(dense_ref, source_ref, target_ref, forward_ref, outer_ref):
    turns, width = source_ref.shape[:2]
    total = jnp.zeros(forward_ref.shape, jnp.float32)
    for turn in range(turns):
        total += jnp.dot(
            dense_ref[:, turn * width : (turn + 1) * width],
            source_ref[turn],
            preferred_element_type=jnp.float32,
        )
    forward = total.astype(forward_ref.dtype)
    forward_ref[...] = forward
    outer_ref[...] = lax.dot_general(
        forward, target_ref[...], (((0,), (0,)), ((), ())), preferred_element_type=jnp.float32
    ).astype(outer_ref.dtype)


def dense_products(dense, sources, targets):
    rows, width = targets.shape
    return pl.pallas_call(
        apply_dense,
        out_shape=(
            jax.ShapeDtypeStruct((rows, width), jnp.bfloat16),
            jax.ShapeDtypeStruct((width, width), jnp.bfloat16),
        ),
        in_specs=[pl.BlockSpec(memory_space=pltpu.VMEM)] * 3,
        out_specs=[pl.BlockSpec(memory_space=pltpu.VMEM)] * 2,
        compiler_params=pltpu.CompilerParams(vmem_limit_bytes=24 * 1024 * 1024),
        name="apply_dense",
    )(dense, sources, targets)


def dense_block(masks, places, count, rows, cols):
    slots = masks.shape[0]
    return pl.pallas_call(
        place_tiles,
        out_shape=jax.ShapeDtypeStruct((rows, cols), jnp.bfloat16),
        grid_spec=pltpu.PrefetchScalarGridSpec(
            num_scalar_prefetch=2,
            grid=(slots // STEP,),
            in_specs=[pl.BlockSpec((STEP, TILE, TILE), lambda i, n, p: (i, 0, 0))],
            out_specs=pl.BlockSpec((rows, cols), lambda i, n, p: (0, 0)),
        ),
        compiler_params=pltpu.CompilerParams(vmem_limit_bytes=16 * 1024 * 1024),
        cost_estimate=pl.CostEstimate(
            flops=slots * TILE * TILE,
            bytes_accessed=slots * TILE * TILE * 4 + rows * cols * 2,
            transcendentals=0,
        ),
        name="place_tiles",
    )(count, places, masks)


def size_of(axes):
    size = 1
    for axis in axes:
        size *= SIZES[axis]
    return size


def copies_of(piece, axes):
    return jnp.broadcast_to(piece[None], (size_of(axes), *piece.shape))


def spread(piece, axes):
    return lax.all_to_all(copies_of(piece, axes), axes, 0, 0)


def swap(pieces, axes):
    return lax.all_to_all(pieces, axes, 0, 0)


def total(pieces):
    return jnp.sum(pieces.astype(jnp.float32), axis=0)


def shifted(piece, axis, step):
    size = SIZES[axis]
    return lax.ppermute(piece, axis, [(i, (i + step) % size) for i in range(size)])


def in_order(blocks, axis, dim):
    size, me = SIZES[axis], lax.axis_index(axis)
    shape = blocks[0].shape[:dim] + (size,) + blocks[0].shape[dim:]
    whole = jnp.zeros(shape, blocks[0].dtype)
    for step, block in enumerate(blocks):
        whole = lax.dynamic_update_index_in_dim(whole, block, (me + size - step) % size, dim)
    return whole


def block_of(pieces, axis, step, dim):
    place = (lax.axis_index(axis) + step) % SIZES[axis]
    return lax.dynamic_index_in_dim(pieces, place, dim, keepdims=False)


def sum_of(blocks):
    whole = blocks[0].astype(jnp.float32)
    for block in blocks[1:]:
        whole = whole + block.astype(jnp.float32)
    return whole.astype(blocks[0].dtype)


def beside(pieces, block):
    return jnp.concatenate(
        [pieces, jnp.broadcast_to(block[None], (pieces.shape[0], *block.shape))], axis=1
    )


def local(features, weight, out_counts, in_counts, tile_mask, tile_pos, tile_count, cotangent):
    bf16, f32 = jnp.bfloat16, jnp.float32
    mine, width = features.shape
    rows = mine * size_of(ROW)
    cols = mine * size_of(COL)
    out_scale = lax.rsqrt(out_counts.astype(f32))[:, None]
    in_scale = lax.rsqrt(in_counts.astype(f32))[:, None]
    scaled = (cotangent.astype(f32) * in_scale).astype(bf16)

    near = swap(scaled_copies(features, out_counts, ("y", "zl")), ("y", "zl"))
    near = near.reshape(-1, width)
    dense = dense_block(tile_mask[0, 0], tile_pos[0, 0], tile_count[0], rows, cols)
    across = in_order([scaled] + [shifted(scaled, "zh", step) for step in (1, 2, 3)], "zh", 0)
    near, across, dense = lax.optimization_barrier((near, across, dense))
    sources = spread(near, ("x",))
    targets = in_order((across, shifted(across, "core", 1)), "core", 1).reshape(rows, width)

    backward = lax.dot_general(
        dense, targets, (((0,), (0,)), ((), ())), preferred_element_type=f32
    ).astype(bf16)
    thirds = backward.reshape(-1, SIZES["zl"], mine, width)
    kept, second, third = (block_of(thirds, "zl", step, 1) for step in range(3))
    second, third = shifted(second, "zl", 1), shifted(third, "zl", 2)

    forward, outer = dense_products(dense, sources, targets)
    outer = copies_of(outer.reshape(SIZES["y"], -1, width), ("core",))
    outer = total(swap(outer.reshape(-1, *outer.shape[2:]), ("core", "y"))).astype(bf16)
    forward = forward.reshape(SIZES["zh"], SIZES["core"], mine, width)
    other = shifted(block_of(forward, "core", 1, 1), "core", 1)
    forward = sum_of((block_of(forward, "core", 0, 1), other))
    outer, second, third, forward = lax.optimization_barrier((outer, second, third, forward))
    part = sum_of((kept, second, third)).reshape(SIZES["x"], -1, mine, width)
    kept, first, second, third = (block_of(part, "x", step, 0) for step in range(4))
    outer = total(spread(outer, ("x", "zl"))).astype(bf16)
    outer, second = lax.optimization_barrier((outer, shifted(second, "x", 2)))
    part = sum_of((kept, shifted(first, "x", 1), second, shifted(third, "x", 3)))
    both = total(swap(beside(forward, outer), ("zh",)))
    forward_mine, outer = both[:mine], both[mine:].astype(bf16)
    output = (
        jnp.dot(forward_mine.astype(bf16), weight, preferred_element_type=f32) * in_scale
    ).astype(bf16)

    last = swap(beside(part, outer), ("y",))
    grad_weight = last[:, mine:].reshape(width, width).astype(f32)
    back_agg = (total(last[:, :mine]) * out_scale).astype(bf16)
    grad_features = lax.dot_general(
        back_agg, weight, (((1,), (1,)), ((), ())), preferred_element_type=f32
    ).astype(bf16)
    return (output, grad_features, grad_weight)


def solution(mesh):
    fine = Mesh(mesh.devices.reshape(tuple(SIZES.values())), tuple(SIZES))
    by_row, by_col = ROW + COL, COL + ROW
    placed = (
        P(by_row, None),
        P(),
        P(by_row),
        P(by_col),
        P(COL, ROW, None, None, None),
        P(COL, ROW, None),
        P(COL, ROW),
        P(by_col, None),
    )
    return jax.shard_map(
        local,
        mesh=fine,
        in_specs=placed,
        out_specs=(P(by_col, None), P(by_row, None), P()),
        check_vma=False,
    )
```

```python
import jax
import jax.numpy as jnp
from jax import lax
from jax.experimental import pallas as pl
from jax.experimental.pallas import tpu as pltpu
from jax.sharding import Mesh, PartitionSpec as P

TILE = 128
STEP = 6
ROW = ("zh", "core")
COL = ("x", "y", "zl")
SIZES = {"zh": 4, "core": 2, "x": 4, "y": 8, "zl": 3}


def place_tiles(count_ref, place_ref, mask_ref, dense_ref):
    step = pl.program_id(0)
    tile_cols = dense_ref.shape[1] // TILE

    @pl.when(step == 0)
    def _():
        dense_ref[...] = jnp.zeros_like(dense_ref)

    for inner in range(STEP):
        slot = step * STEP + inner

        @pl.when(slot < count_ref[0])
        def _():
            place = place_ref[slot]
            row = pl.multiple_of(place // tile_cols * TILE, TILE)
            col = pl.multiple_of(place % tile_cols * TILE, TILE)
            block = mask_ref[inner].astype(jnp.float32).astype(jnp.bfloat16)
            dense_ref[pl.ds(row, TILE), pl.ds(col, TILE)] = block


def scale_copies(count_ref, value_ref, copies_ref):
    nodes = value_ref.shape[0]
    scale = lax.rsqrt(count_ref[...].astype(jnp.float32))
    here = lax.broadcasted_iota(jnp.int32, (nodes, nodes), 0)
    there = lax.broadcasted_iota(jnp.int32, (nodes, nodes), 1)
    scale = jnp.broadcast_to(scale, (nodes, nodes))
    scale = jnp.sum(jnp.where(here == there, scale, 0.0), axis=1, keepdims=True)
    scaled = (value_ref[...].astype(jnp.float32) * scale).astype(copies_ref.dtype)
    for copy in range(copies_ref.shape[0]):
        copies_ref[copy] = scaled


def scaled_copies(values, counts, axes):
    return pl.pallas_call(
        scale_copies,
        out_shape=jax.ShapeDtypeStruct((size_of(axes), *values.shape), values.dtype),
        in_specs=[pl.BlockSpec(memory_space=pltpu.VMEM)] * 2,
        out_specs=pl.BlockSpec(memory_space=pltpu.VMEM),
        name="scale_copies",
    )(counts.reshape(1, -1), values)


def apply_dense(dense_ref, source_ref, target_ref, forward_ref, outer_ref):
    turns, width = source_ref.shape[:2]
    total = jnp.zeros(forward_ref.shape, jnp.float32)
    for turn in range(turns):
        total += jnp.dot(
            dense_ref[:, turn * width : (turn + 1) * width],
            source_ref[turn],
            preferred_element_type=jnp.float32,
        )
    forward = total.astype(forward_ref.dtype)
    forward_ref[...] = forward
    outer_ref[...] = lax.dot_general(
        forward, target_ref[...], (((0,), (0,)), ((), ())), preferred_element_type=jnp.float32
    ).astype(outer_ref.dtype)


def dense_products(dense, sources, targets):
    rows, width = targets.shape
    return pl.pallas_call(
        apply_dense,
        out_shape=(
            jax.ShapeDtypeStruct((rows, width), jnp.bfloat16),
            jax.ShapeDtypeStruct((width, width), jnp.bfloat16),
        ),
        in_specs=[pl.BlockSpec(memory_space=pltpu.VMEM)] * 3,
        out_specs=[pl.BlockSpec(memory_space=pltpu.VMEM)] * 2,
        compiler_params=pltpu.CompilerParams(vmem_limit_bytes=24 * 1024 * 1024),
        name="apply_dense",
    )(dense, sources, targets)


def dense_block(masks, places, count, rows, cols):
    slots = masks.shape[0]
    return pl.pallas_call(
        place_tiles,
        out_shape=jax.ShapeDtypeStruct((rows, cols), jnp.bfloat16),
        grid_spec=pltpu.PrefetchScalarGridSpec(
            num_scalar_prefetch=2,
            grid=(slots // STEP,),
            in_specs=[pl.BlockSpec((STEP, TILE, TILE), lambda i, n, p: (i, 0, 0))],
            out_specs=pl.BlockSpec((rows, cols), lambda i, n, p: (0, 0)),
        ),
        compiler_params=pltpu.CompilerParams(vmem_limit_bytes=16 * 1024 * 1024),
        cost_estimate=pl.CostEstimate(
            flops=slots * TILE * TILE,
            bytes_accessed=slots * TILE * TILE * 4 + rows * cols * 2,
            transcendentals=0,
        ),
        name="place_tiles",
    )(count, places, masks)


def size_of(axes):
    size = 1
    for axis in axes:
        size *= SIZES[axis]
    return size


def copies_of(piece, axes):
    return jnp.broadcast_to(piece[None], (size_of(axes), *piece.shape))


def spread(piece, axes):
    return lax.all_to_all(copies_of(piece, axes), axes, 0, 0)


def swap(pieces, axes):
    return lax.all_to_all(pieces, axes, 0, 0)


def total(pieces):
    return jnp.sum(pieces.astype(jnp.float32), axis=0)


def shifted(piece, axis, step):
    size = SIZES[axis]
    return lax.ppermute(piece, axis, [(i, (i + step) % size) for i in range(size)])


def in_order(blocks, axis, dim):
    size, me = SIZES[axis], lax.axis_index(axis)
    shape = blocks[0].shape[:dim] + (size,) + blocks[0].shape[dim:]
    whole = jnp.zeros(shape, blocks[0].dtype)
    for step, block in enumerate(blocks):
        whole = lax.dynamic_update_index_in_dim(whole, block, (me + size - step) % size, dim)
    return whole


def block_of(pieces, axis, step, dim):
    place = (lax.axis_index(axis) + step) % SIZES[axis]
    return lax.dynamic_index_in_dim(pieces, place, dim, keepdims=False)


def sum_of(blocks):
    whole = blocks[0].astype(jnp.float32)
    for block in blocks[1:]:
        whole = whole + block.astype(jnp.float32)
    return whole.astype(blocks[0].dtype)


def beside(pieces, block):
    return jnp.concatenate(
        [pieces, jnp.broadcast_to(block[None], (pieces.shape[0], *block.shape))], axis=1
    )


def local(features, weight, out_counts, in_counts, tile_mask, tile_pos, tile_count, cotangent):
    bf16, f32 = jnp.bfloat16, jnp.float32
    mine, width = features.shape
    rows = mine * size_of(ROW)
    cols = mine * size_of(COL)
    out_scale = lax.rsqrt(out_counts.astype(f32))[:, None]
    in_scale = lax.rsqrt(in_counts.astype(f32))[:, None]
    scaled = (cotangent.astype(f32) * in_scale).astype(bf16)

    near = swap(scaled_copies(features, out_counts, ("y", "zl")), ("y", "zl"))
    near = near.reshape(-1, width)
    dense = dense_block(tile_mask[0, 0], tile_pos[0, 0], tile_count[0], rows, cols)
    across = in_order([scaled] + [shifted(scaled, "zh", step) for step in (1, 2, 3)], "zh", 0)
    near, across, dense = lax.optimization_barrier((near, across, dense))
    sources = spread(near, ("x",))
    targets = in_order((across, shifted(across, "core", 1)), "core", 1).reshape(rows, width)

    backward = lax.dot_general(
        dense, targets, (((0,), (0,)), ((), ())), preferred_element_type=f32
    ).astype(bf16)
    quarters = backward.reshape(SIZES["x"], -1, width)
    kept, *sent = (block_of(quarters, "x", step, 0) for step in range(4))
    sent = [shifted(block, "x", step + 1) for step, block in enumerate(sent)]

    forward, outer = dense_products(dense, sources, targets)
    outer = swap(outer.reshape(SIZES["y"], -1, width), ("y",))
    outer = total(outer).astype(bf16)
    forward = forward.reshape(SIZES["zh"], SIZES["core"], mine, width)
    other = shifted(block_of(forward, "core", 1, 1), "core", 1)
    forward = sum_of((block_of(forward, "core", 0, 1), other))
    outer, sent = lax.optimization_barrier((outer, sent))
    part = sum_of([kept, *sent]).reshape(SIZES["y"], SIZES["zl"], mine, width)
    kept, second, third = (block_of(part, "zl", step, 1) for step in range(3))
    outer = total(spread(outer, ("core", "x", "zl"))).astype(bf16)
    part = sum_of((kept, shifted(second, "zl", 1), shifted(third, "zl", 2)))
    both = total(swap(beside(forward, outer), ("zh",)))
    forward_mine, outer = both[:mine], both[mine:].astype(bf16)
    output = (
        jnp.dot(forward_mine.astype(bf16), weight, preferred_element_type=f32) * in_scale
    ).astype(bf16)

    last = swap(beside(part, outer), ("y",))
    grad_weight = last[:, mine:].reshape(width, width).astype(f32)
    back_agg = (total(last[:, :mine]) * out_scale).astype(bf16)
    grad_features = lax.dot_general(
        back_agg, weight, (((1,), (1,)), ((), ())), preferred_element_type=f32
    ).astype(bf16)
    return (output, grad_features, grad_weight)


def solution(mesh):
    fine = Mesh(mesh.devices.reshape(tuple(SIZES.values())), tuple(SIZES))
    by_row, by_col = ROW + COL, COL + ROW
    placed = (
        P(by_row, None),
        P(),
        P(by_row),
        P(by_col),
        P(COL, ROW, None, None, None),
        P(COL, ROW, None),
        P(COL, ROW),
        P(by_col, None),
    )
    return jax.shard_map(
        local,
        mesh=fine,
        in_specs=placed,
        out_specs=(P(by_col, None), P(by_row, None), P()),
        check_vma=False,
    )
```
